32 devices in a mesh: seq: 8 (over z, y), exp: 4 (over x, core).
Axes of the slice: x: 2, y: 2, z: 4, core: 2. Of those that a mesh axis runs over, the one named last changes fastest.
Arguments:
- query_proj: bfloat16 [2048, 2048], P('seq', 'exp'), may hold values from -6 to 6
- key_proj: bfloat16 [2048, 2048], P('seq', 'exp'), may hold values from -6 to 6
- value_proj: bfloat16 [2048, 4096], P('seq', 'exp'), may hold values from -6 to 6
- result_valve_maps: bfloat16 [2048, 4096], P('seq', 'exp'), may hold values from -6 to 6
- beta_logit: float32 [2048, 32], P('seq', 'exp'), may hold values from -12 to 3
- decay_logit: float32 [2048, 32], P('seq', 'exp'), may hold values from -8 to 4126
- decay_rate: float32 [32], P('exp'), may hold values from 0 to 0.06
- conv_query: float32 [4, 2048], P(None, 'exp'), may hold values from -3 to 3
- conv_key: float32 [4, 2048], P(None, 'exp'), may hold values from -3 to 3
- conv_value: float32 [4, 4096], P(None, 'exp'), may hold values from -3 to 3
- norm_gain: float32 [128], replicated, may hold values from 0.1 to 1.9
- output_weight: bfloat16 [4096, 2048], P('exp'), may hold values from -0.09375 to 0.09375
- residual: bfloat16 [2048, 2048], P(('seq', 'exp')), may hold values from -6 to 6
- post_gain: float32 [2048], replicated, may hold values from 0.1 to 1.9
- route_experts: int32 [2048, 10], P(('seq', 'exp')), may hold values from 0 to 63, all different within a row; in each aligned block of 64 rows (0 to 63, 64 to 127, ...) at most 20 rows name the same one
- route_weights: float32 [2048, 10], P(('seq', 'exp')), may hold values from 0.05 to 1
- expert_gate: bfloat16 [64, 2048, 512], P(('seq', 'exp')), may hold values from -0.125 to 0.125
- expert_up: bfloat16 [64, 2048, 512], P(('seq', 'exp')), may hold values from -0.125 to 0.125
- expert_down: bfloat16 [64, 512, 2048], P(('seq', 'exp')), may hold values from -0.25 to 0.25
Outputs:
- mixer_out: bfloat16 [2048, 2048], P(('seq', 'exp'))
- expert_mixture: bfloat16 [2048, 2048], P(('seq', 'exp'))
The draws below stay inside these ranges and needn't reach their ends.
Inputs may be any that keep to these rules, and one draw needn't show every extreme that they name: `route_experts`: each row names 10 different experts. Within the 64 rows of one device (aligned blocks of 64 rows) no expert is named more than 20 times, and in every draw some device names some expert exactly 20 times.
All inputs are finite; a program needn't handle non-finite values.
Results may differ from the reference program's by a relative error of at most 0.02.
Values may be sent and summed in bfloat16 or wider, within the bound.
A program may use at most 128 MiB of HBM per device.

```python
import math
import jax
import jax.numpy as jnp
import numpy as np
from jax import lax

D = 2048
KEY_HEADS = 16
VAL_HEADS = 32
HEAD_DIM = 128
KCONV = 4
FF = 512
TOPK = 10
BLOCK = 64
TOK_DEV = 256
KD = 2048
VD = 4096
TOKENS = 2048
MOE_ROWS = 64
EXPERTS = 64
CAP = 20
N_SEQ = 8
N_EXP = 4


def slow_heads(key):
    shuffled = jax.random.permutation(jax.random.fold_in(key, 101), VAL_HEADS)
    keeping = VAL_HEADS // 2
    return shuffled < keeping


def head_rates(key):
    slow = slow_heads(key)
    uniform_draw = jax.random.uniform(jax.random.fold_in(key, 102), (VAL_HEADS,), jnp.float32)
    slow_rate = (0.5 + uniform_draw) / TOKENS
    fast_rate = 0.03 + 0.03 * uniform_draw
    return jnp.where(slow, slow_rate, fast_rate)


def draw_decay_rate(key, part):
    return head_rates(key).astype(jnp.float32)


def draw_decay_logit(key, part):
    rates = head_rates(key)
    blocks = TOKENS // TOK_DEV
    offsets = jax.random.uniform(jax.random.fold_in(key, 103), (blocks, VAL_HEADS), jnp.float32, -1.0, 1.0)
    jitter = jnp.clip(jax.random.normal(jax.random.fold_in(key, 104), (TOKENS, VAL_HEADS), jnp.float32), -5.0, 5.0)
    starting_shift = jnp.repeat(offsets, TOK_DEV, axis=0) + jitter
    spots = jax.random.randint(jax.random.fold_in(key, 105), (4, VAL_HEADS), 0, TOKENS)
    kept = jax.random.uniform(jax.random.fold_in(key, 106), (4, VAL_HEADS), jnp.float32, 0.5, 0.8)
    target = -jnp.log(kept) / rates[None, :]
    reciprocal_operator = target + jnp.log(-jnp.expm1(-target))
    place_locator = jnp.arange(TOKENS)[:, None, None] == spots[None, :, :]
    dispatch_batch = jnp.sum(jnp.where(place_locator, reciprocal_operator[None, :, :], 0.0), axis=1)
    removed_elements = jnp.any(place_locator, axis=1)
    return jnp.where(removed_elements, dispatch_batch, starting_shift).astype(jnp.float32)


def draw_beta_logit(key, part):
    slow = slow_heads(key)
    center = jnp.where(slow, jnp.log(48.0 / TOKENS), 0.0)
    jitter = 0.5 * jnp.clip(jax.random.normal(jax.random.fold_in(key, 107), (TOKENS, VAL_HEADS), jnp.float32), -5.0, 5.0)
    return (center[None, :] + jitter).astype(jnp.float32)


def steps_of(key, dims, pieces, smallest, largest):
    level = 1.0
    for axis_at, parts in pieces:
        draws = jax.random.uniform(jax.random.fold_in(jax.random.fold_in(key, 6), axis_at), (parts,), jnp.float32, smallest / len(pieces), largest / len(pieces))
        level = level * jnp.repeat(jnp.exp(draws), dims[axis_at] // parts).reshape((-1,) + (1,) * (len(dims) - 1 - axis_at))
    return level


def shared_out(own_key, own, number, rows, count, top, limit, skew):
    order = jax.random.permutation(own_key, count)
    packed, ordinary = load_shares(count, rows * top, limit, skew, True), load_shares(count, rows * top, limit, skew, False)
    places = jnp.arange(count)

    def named(tallies, offset_by):
        used = int((tallies > 0).sum())
        fixed = max(1, used // 4)
        shifted = fixed + (places - fixed + offset_by * (used - fixed)) % max(1, count - fixed)
        return jnp.zeros((count,), jnp.int32).at[order[jnp.where(places < fixed, places, shifted)]].set(jnp.asarray(tallies, jnp.int32))

    tallies = jnp.where(number % 4 == 0, named(packed, number // 4), named(ordinary, number - number // 4 - 1))
    mixed = jax.random.permutation(jax.random.fold_in(own, 3), count)
    donor, receiver = mixed[0:count // 2 * 2:2], mixed[1:count // 2 * 2:2]
    margin = jnp.minimum(tallies[donor] - 1, limit - tallies[receiver]) // 2
    margin = jnp.where((donor == order[0]) | (receiver == order[0]) | (tallies[receiver] == 0), 0, jnp.maximum(margin, 0))
    shifted = jax.random.randint(jax.random.fold_in(own, 4), (count // 2,), 0, 1 << 20) % (margin + 1)
    tallies = tallies.at[donor].add(-shifted).at[receiver].add(shifted)
    items = jnp.searchsorted(jnp.cumsum(tallies), jnp.arange(rows * top), side="right").astype(jnp.int32)
    listing = items.reshape(top, rows).T
    listing = listing[jax.random.permutation(jax.random.fold_in(own, 1), rows)]
    offset_by = jax.random.randint(jax.random.fold_in(own, 2), (rows, 1), 0, top)
    return jnp.take_along_axis(listing, (jnp.arange(top)[None, :] + offset_by) % top, axis=1)


def load_shares(count, total, reach, skew, full):
    portions = [(1 << 20) // math.isqrt(grade ** skew) + 1 for grade in range(1, count + 1)]
    largest = reach if full else min(reach, max(-(-total // count), total * portions[0] // sum(portions)))
    least = 1 if total - largest >= count - 1 else 0
    holding, rest = [largest] + [least] * (count - 1), total - largest - least * (count - 1)
    while rest > 0:
        free = [i for i in range(1, count) if holding[i] < largest] or [i for i in range(1, count) if holding[i] < reach]
        mass, remaining = sum([portions[i] for i in free]), rest
        for i in free:
            extra = min(reach - holding[i], max(1, remaining * portions[i] // mass), rest)
            holding[i] = holding[i] + extra
            rest = rest - extra
    return np.array(holding)


def centred(key, extent, deviation, reach, pieces=(), held_as=jnp.bfloat16):
    drawn = jax.random.normal(key, extent, jnp.float32) * deviation
    if len(pieces) > 0:
        drawn = steps_of(key, extent, pieces, -0.22, 0.18) * drawn
    return jnp.clip(drawn, min=-reach, max=reach).astype(held_as)


def setup_inputs(seed: int = 0) -> dict:
    key_list = jax.random.split(jax.random.key(seed), 20)
    query_proj = centred(key_list[0], (TOKENS, KD), 1.0, 6.0, ((0, 8), (1, 4)))
    key_proj = centred(key_list[1], (TOKENS, KD), 1.0, 6.0, ((0, 8), (1, 4)))
    value_proj = centred(key_list[2], (TOKENS, VD), 1.0, 6.0, ((0, 8), (1, 4)))
    result_valve_maps = centred(key_list[3], (TOKENS, VD), 1.0, 6.0, ((0, 8), (1, 4)))
    beta_logit = draw_beta_logit(jax.random.fold_in(key_list[19], 71), 0)
    decay_logit = draw_decay_logit(jax.random.fold_in(key_list[19], 71), 0)
    decay_rate = draw_decay_rate(jax.random.fold_in(key_list[19], 71), 0)
    conv_query = centred(key_list[7], (KCONV, KD), KCONV ** -0.5, 3.0, ((1, 4),), jnp.float32)
    conv_key = centred(key_list[8], (KCONV, KD), KCONV ** -0.5, 3.0, ((1, 4),), jnp.float32)
    conv_value = centred(key_list[9], (KCONV, VD), KCONV ** -0.5, 3.0, ((1, 4),), jnp.float32)
    norm_gain = jnp.clip(1.0 + 0.18 * jax.random.normal(key_list[10], (HEAD_DIM,), jnp.float32), 0.1, 1.9)
    output_weight = centred(key_list[11], (VD, D), VD ** -0.5, 0.09375, ((0, 4),))
    residual = centred(key_list[12], (TOKENS, D), 1.0, 6.0, ((0, 32),))
    post_gain = jnp.clip(1.0 + 0.18 * jax.random.normal(key_list[13], (D,), jnp.float32), 0.1, 1.9)
    route_experts_keys = jax.random.split(jax.random.fold_in(key_list[14], 1), TOKENS // MOE_ROWS)
    route_experts_turns = jax.random.permutation(jax.random.fold_in(key_list[14], 3), TOKENS // MOE_ROWS)
    route_experts = jax.vmap(lambda own, number: shared_out(jax.random.fold_in(key_list[14], 2), own, number, MOE_ROWS, EXPERTS, TOPK, CAP, 2))(route_experts_keys, route_experts_turns).reshape((TOKENS, TOPK))
    route_weights = jnp.clip(jnp.exp(math.log(1.0) - 2.9957323 * jax.random.uniform(key_list[15], (TOKENS, TOPK), jnp.float32) ** steps_of(key_list[15], (TOKENS, TOPK), ((0, 32),), -0.2, 0.2)), 0.05, 1.0)
    expert_gate = centred(key_list[16], (EXPERTS, D, FF), D ** -0.5, 0.125, ((0, 32),))
    expert_up = centred(key_list[17], (EXPERTS, D, FF), D ** -0.5, 0.125, ((0, 32),))
    expert_down = centred(key_list[18], (EXPERTS, FF, D), FF ** -0.5, 0.25, ((0, 32),))
    return {"query_proj": query_proj, "key_proj": key_proj, "value_proj": value_proj, "result_valve_maps": result_valve_maps, "beta_logit": beta_logit, "decay_logit": decay_logit, "decay_rate": decay_rate, "conv_query": conv_query, "conv_key": conv_key, "conv_value": conv_value, "norm_gain": norm_gain, "output_weight": output_weight, "residual": residual, "post_gain": post_gain, "route_experts": route_experts, "route_weights": route_weights, "expert_gate": expert_gate, "expert_up": expert_up, "expert_down": expert_down}


highest = lax.Precision.HIGHEST
epsilon = 1e-06

def causal_conv(value_rows, kernel, leading):
    padded = jnp.concatenate([leading, value_rows], axis=0)
    length = value_rows.shape[0]
    running = jnp.zeros_like(value_rows)
    for offset in range(kernel.shape[0]):
        running = running + kernel[offset] * padded[offset:offset + length]
    return jax.nn.silu(running)

def block_terms(queries, key_rows, value_rows, beta_gate, log_decay):
    block_size = queries.shape[-2]
    cumulative = jnp.cumsum(log_decay, axis=-1)
    spread = cumulative[..., :, None] - cumulative[..., None, :]
    row_index = lax.broadcasted_iota(jnp.int32, (block_size, block_size), 0)
    col_index = lax.broadcasted_iota(jnp.int32, (block_size, block_size), 1)
    lower_mask = row_index >= col_index
    strict = row_index > col_index
    decay_mask = jnp.where(lower_mask, jnp.exp(jnp.where(lower_mask, spread, 0.0)), 0.0)
    key_key = jnp.einsum('...id,...jd->...ij', key_rows, key_rows, precision=highest)
    coupling = jnp.where(strict, beta_gate[..., :, None] * key_key * decay_mask, 0.0)
    identity = jnp.eye(block_size, dtype=jnp.float32)
    growth = jnp.exp(cumulative)
    stacked = jnp.concatenate([beta_gate[..., None] * value_rows, (beta_gate * growth)[..., None] * key_rows], axis=-1)
    solved = jax.scipy.linalg.solve_triangular(identity + coupling, stacked, lower=True, unit_diagonal=True)
    payload_width = value_rows.shape[-1]
    updates = solved[..., :payload_width]
    key_mix = solved[..., payload_width:]
    scores = jnp.einsum('...id,...jd->...ij', queries, key_rows, precision=highest) * decay_mask
    local_out = jnp.einsum('...ij,...jv->...iv', scores, updates, precision=highest)
    lifted = growth[..., None] * queries - jnp.einsum('...ij,...jd->...id', scores, key_mix, precision=highest)
    remain = jnp.exp(cumulative[..., -1:] - cumulative)
    key_tail = key_rows * remain[..., None]
    key_dim = key_rows.shape[-1]
    carry_map = jnp.exp(cumulative[..., -1])[..., None, None] * jnp.eye(key_dim, dtype=jnp.float32) - jnp.einsum('...ci,...cj->...ij', key_mix, key_tail, precision=highest)
    write_term = jnp.einsum('...cv,...ck->...vk', updates, key_tail, precision=highest)
    return (local_out, lifted, carry_map, write_term)

def head_chain(head_inputs):
    queries, key_rows, value_rows, beta_gate, log_decay = head_inputs
    local_out, lifted, carry_map, write_term = block_terms(queries, key_rows, value_rows, beta_gate, log_decay)

    def advance(memory, block_item):
        block_out, block_lift, block_map, block_write = block_item
        result = block_out + jnp.einsum('cd,vd->cv', block_lift, memory, precision=highest)
        memory = jnp.einsum('vd,de->ve', memory, block_map, precision=highest) + block_write
        return (memory, result)
    initial = jnp.zeros((value_rows.shape[-1], key_rows.shape[-1]), jnp.float32)
    _, outputs = lax.scan(advance, initial, (local_out, lifted, carry_map, write_term))
    return outputs

def reference(query_proj, key_proj, value_proj, result_valve_maps, beta_logit, decay_logit, decay_rate, conv_query, conv_key, conv_value, norm_gain, output_weight, residual, post_gain, route_experts, route_weights, expert_gate, expert_up, expert_down):
    rim_width = KCONV - 1
    query_conv = causal_conv(query_proj.astype(jnp.float32), conv_query, jnp.zeros((rim_width, KD), jnp.float32))
    key_conv = causal_conv(key_proj.astype(jnp.float32), conv_key, jnp.zeros((rim_width, KD), jnp.float32))
    value_conv = causal_conv(value_proj.astype(jnp.float32), conv_value, jnp.zeros((rim_width, VD), jnp.float32))
    key_split = key_conv.reshape(TOKENS, KEY_HEADS, HEAD_DIM)
    key_unit = key_split * lax.rsqrt(lax.optimization_barrier(jnp.sum(key_split * key_split, axis=-1, keepdims=True)) + epsilon)
    query_rep = jnp.repeat(query_conv.reshape(TOKENS, KEY_HEADS, HEAD_DIM), 2, axis=1)
    key_rep = jnp.repeat(key_unit, 2, axis=1)
    value_split = value_conv.reshape(TOKENS, VAL_HEADS, HEAD_DIM)
    beta_gate = jax.nn.sigmoid(beta_logit)
    log_decay = -decay_rate[None, :] * jax.nn.softplus(decay_logit)
    blocks = TOKENS // BLOCK

    def arrange(array):
        return array.reshape(blocks, BLOCK, VAL_HEADS, HEAD_DIM).transpose(2, 0, 1, 3)

    def arrange_gate(array):
        return array.reshape(blocks, BLOCK, VAL_HEADS).transpose(2, 0, 1)
    core = lax.map(head_chain, (arrange(query_rep), arrange(key_rep), arrange(value_split), arrange_gate(beta_gate), arrange_gate(log_decay)))
    core = core.transpose(1, 2, 0, 3).reshape(TOKENS, VAL_HEADS, HEAD_DIM)
    gate_heads = result_valve_maps.astype(jnp.float32).reshape(TOKENS, VAL_HEADS, HEAD_DIM)
    mean_square = lax.optimization_barrier(jnp.mean(core * core, axis=-1, keepdims=True))
    normed = (core * lax.rsqrt(mean_square + epsilon) * norm_gain * jax.nn.silu(gate_heads)).astype(jnp.bfloat16).reshape(TOKENS, VD)
    mixer = jnp.dot(normed.astype(jnp.float32), output_weight.astype(jnp.float32), preferred_element_type=jnp.float32)
    mixer_out = (residual.astype(jnp.float32) + mixer).astype(jnp.bfloat16)
    mixed = mixer_out.astype(jnp.float32)
    moe_in = (mixed * lax.rsqrt(lax.optimization_barrier(jnp.mean(mixed * mixed, axis=-1, keepdims=True)) + epsilon) * post_gain).astype(jnp.bfloat16)
    shares = route_weights / lax.optimization_barrier(jnp.sum(route_weights, axis=1, keepdims=True))
    linear_labels = route_experts.reshape(-1).astype(jnp.int32)
    flat_shares = shares.reshape(-1)
    pick_order = jnp.argsort(linear_labels, stable=True).astype(jnp.int32)
    counts = jax.ops.segment_sum(jnp.ones_like(linear_labels), linear_labels, num_segments=EXPERTS).astype(jnp.int32)
    starts = (jnp.cumsum(counts) - counts).astype(jnp.int32)
    window = CAP * N_SEQ * N_EXP
    order_padded = jnp.concatenate([pick_order, jnp.zeros((window,), jnp.int32)])

    def add_expert(summed_total, expert_item):
        gate_matrix, up_matrix, down_matrix, expert = expert_item
        picked = lax.dynamic_slice(order_padded, (starts[expert].astype(jnp.int32),), (window,))
        live_mask = jnp.arange(window, dtype=jnp.int32) < counts[expert]
        token_rows = (picked // TOPK).astype(jnp.int32)
        inputs = moe_in[token_rows]
        gate_act = jnp.dot(inputs.astype(jnp.float32), gate_matrix.astype(jnp.float32), preferred_element_type=jnp.float32)
        up_act = jnp.dot(inputs.astype(jnp.float32), up_matrix.astype(jnp.float32), preferred_element_type=jnp.float32)
        inner = (jax.nn.silu(gate_act) * up_act).astype(jnp.bfloat16)
        expert_res = jnp.dot(inner.astype(jnp.float32), down_matrix.astype(jnp.float32), preferred_element_type=jnp.float32).astype(jnp.bfloat16)
        contrib = jnp.where(live_mask[:, None], flat_shares[picked][:, None] * expert_res.astype(jnp.float32), 0.0)
        return (summed_total.at[token_rows].add(contrib), None)
    summed_total, _ = lax.scan(add_expert, jnp.zeros((TOKENS, D), jnp.float32), (expert_gate, expert_up, expert_down, jnp.arange(EXPERTS, dtype=jnp.int32)))
    expert_mixture = summed_total.astype(jnp.bfloat16)
    return (mixer_out, expert_mixture)
```

```python
import functools

import jax
import jax.numpy as jnp
from jax import lax
from jax.experimental import pallas as pl
from jax.experimental.pallas import tpu as pltpu
from jax.sharding import PartitionSpec as P

epsilon = 1e-06
f32 = jnp.float32
bf16 = jnp.bfloat16
MESH = pl.DeviceIdType.MESH
NN = (((1,), (0,)), ((), ()))
NT = (((1,), (1,)), ((), ()))
TN = (((0,), (0,)), ((), ()))
VMEM = pl.BlockSpec(memory_space=pltpu.VMEM)
ANY = pl.BlockSpec(memory_space=pl.ANY)


def shifted(value, axis, steps):
    count = lax.axis_size(axis)
    leading, last = (max(0, -steps), min(count, count - steps))
    return lax.ppermute(value, axis, [(source, source + steps) for source in range(leading, last)])


def silu(x):
    return x / (1.0 + jnp.exp(-x))


def mm(a, b, dims=NN):
    return lax.dot_general(a, b, dims, preferred_element_type=f32)


def split(x):
    high = x.astype(bf16)
    return high, (x - high.astype(f32)).astype(bf16)


def dot3(a, b, dims=NN):
    ah, al = split(a)
    bh, bl = split(b)
    return mm(ah, bh, dims) + (mm(ah, bl, dims) + mm(al, bh, dims))


def conv_act(x_ref, halo_ref, w_ref):
    taps = w_ref.shape[0]
    rows = x_ref.shape[0]
    top = halo_ref.shape[0]
    padded = jnp.concatenate([halo_ref[...], x_ref[...].astype(f32)], axis=0)
    total = w_ref[taps - 1 : taps, :] * padded[top : top + rows]
    for j in range(taps - 1):
        start = top - (taps - 1) + j
        total = total + w_ref[j : j + 1, :] * padded[start : start + rows]
    return silu(total)


def local_kernel(
    hd, q_ref, k_ref, v_ref, hq_ref, hk_ref, hv_ref, wq_ref, wk_ref, wv_ref,
    beta_ref, cum_ref, cumt_ref, lo_ref, lift_ref, map_ref, write_ref, coup, inv, score,
):
    rows = q_ref.shape[0]
    key_heads = q_ref.shape[1] // hd
    heads = v_ref.shape[1] // hd
    per = heads // key_heads
    q = conv_act(q_ref, hq_ref, wq_ref)
    k = conv_act(k_ref, hk_ref, wk_ref)
    v = conv_act(v_ref, hv_ref, wv_ref)
    ri = lax.broadcasted_iota(jnp.int32, (rows, rows), 0)
    ci = lax.broadcasted_iota(jnp.int32, (rows, rows), 1)
    apart = ri ^ ci
    low = ri >= ci
    strict = ri > ci
    qs, ks = [], []
    for a in range(key_heads):
        ka = k[:, a * hd : (a + 1) * hd]
        ka = ka * lax.rsqrt(jnp.sum(ka * ka, axis=1, keepdims=True) + epsilon)
        qa = q[:, a * hd : (a + 1) * hd]
        qs.append(qa)
        ks.append(ka)
        kk = dot3(ka, ka, NT)
        qk = dot3(qa, ka, NT)
        for h in range(a * per, (a + 1) * per):
            spread = (cum_ref[:, h : h + 1] - cumt_ref[h : h + 1, :]) + (
                cum_ref[:, heads + h : heads + h + 1] - cumt_ref[heads + h : heads + h + 1, :]
            )
            decay = jnp.where(low, jnp.exp(jnp.where(low, spread, 0.0)), 0.0)
            coupling = jnp.where(strict, beta_ref[:, h : h + 1] * kk * decay, 0.0)
            coup[h] = coupling
            score[h] = qk * decay
            inv[h] = jnp.where(ri == ci, 1.0, 0.0) - jnp.where(apart == 1, coupling, 0.0)

    half = rows // 2
    near_bits = apart[:half, :half]

    def level(step, carry):
        near = lax.shift_right_logical(near_bits, jnp.full_like(near_bits, step)) == 1
        for h in range(heads):
            for part in (slice(0, half), slice(half, rows)):
                x = inv[h, part, part]
                c = jnp.where(near, coup[h, part, part], 0.0)
                inv[h, part, part] = x - dot3(x, dot3(c, x))
        return carry

    lax.fori_loop(1, (half - 1).bit_length(), level, 0)
    for h in range(heads):
        inv[h, half:, :half] = -dot3(inv[h, half:, half:], dot3(coup[h, half:, :half], inv[h, :half, :half]))
    eye = jnp.where(
        lax.broadcasted_iota(jnp.int32, (hd, hd), 0) == lax.broadcasted_iota(jnp.int32, (hd, hd), 1), 1.0, 0.0
    )
    for h in range(heads):
        cum = cum_ref[:, h : h + 1] + cum_ref[:, heads + h : heads + h + 1]
        growth = jnp.exp(cum)
        last_w = cum_ref[rows - 1 : rows, h : h + 1]
        last_f = cum_ref[rows - 1 : rows, heads + h : heads + h + 1]
        remain = jnp.exp(
            (last_w - cum_ref[:, h : h + 1]) + (last_f - cum_ref[:, heads + h : heads + h + 1])
        )
        beta = beta_ref[:, h : h + 1]
        qa, ka = qs[h // per], ks[h // per]
        stacked = jnp.concatenate([beta * v[:, h * hd : (h + 1) * hd], (beta * growth) * ka], axis=1)
        solved = dot3(inv[h], stacked)
        mixed = dot3(score[h], solved)
        lo_ref[:, h * hd : (h + 1) * hd] = mixed[:, :hd]
        lift_ref[:, h * hd : (h + 1) * hd] = growth * qa - mixed[:, hd:]
        ends = dot3(solved, ka * remain, TN)
        write_ref[h] = ends[:hd]
        map_ref[h] = jnp.exp(last_w + last_f) * eye - ends[hd:]


def local_terms(q, k, v, halo, wq, wk, wv, beta, log_decay, hd):
    rows, kc = q.shape
    vc = v.shape[1]
    heads = vc // hd
    groups = 2 if (kc // hd) % 2 == 0 else 1
    gh = heads // groups
    kw, vw = kc // groups, vc // groups
    bounded = jnp.maximum(log_decay, -110.0)
    whole = jnp.floor(bounded)
    sums = jnp.cumsum(jnp.stack([whole, bounded - whole]), axis=1)
    cum = sums.reshape(2, rows, groups, gh).transpose(2, 1, 0, 3).reshape(groups, rows, 2 * gh)
    cumt = sums.reshape(2, rows, groups, gh).transpose(2, 0, 3, 1).reshape(groups, 2 * gh, rows)
    betag = beta.reshape(rows, groups, gh).transpose(1, 0, 2)
    taps = wq.shape[0]
    halo = jnp.concatenate([jnp.zeros((8 - halo.shape[0], halo.shape[1]), f32), halo], axis=0)
    hq, hk, hv = halo[:, :kc], halo[:, kc : 2 * kc], halo[:, 2 * kc :]
    col = lambda r, w: pl.BlockSpec((r, w), lambda g: (0, g))
    lead = lambda a, b: pl.BlockSpec((None, a, b), lambda g: (g, 0, 0))
    mats = pl.BlockSpec((gh, hd, hd), lambda g: (g, 0, 0))
    return pl.pallas_call(
        functools.partial(local_kernel, hd),
        grid=(groups,),
        in_specs=[
            col(rows, kw), col(rows, kw), col(rows, vw), col(8, kw), col(8, kw), col(8, vw),
            col(taps, kw), col(taps, kw), col(taps, vw),
            lead(rows, gh), lead(rows, 2 * gh), lead(2 * gh, rows),
        ],
        out_specs=[col(rows, vw), col(rows, vw), mats, mats],
        out_shape=[
            jax.ShapeDtypeStruct((rows, vc), f32),
            jax.ShapeDtypeStruct((rows, vc), f32),
            jax.ShapeDtypeStruct((heads, hd, hd), f32),
            jax.ShapeDtypeStruct((heads, hd, hd), f32),
        ],
        scratch_shapes=[pltpu.VMEM((gh, rows, rows), f32)] * 3,
        compiler_params=pltpu.CompilerParams(vmem_limit_bytes=60 << 20),
        name="block_terms",
    )(q, k, v, hq, hk, hv, wq, wk, wv, betag, cum, cumt)


def mixer_kernel(
    ns, ne, gather, lo_ref, lift_ref, map_ref, write_ref, valve_ref, gain_ref, w_ref, res_ref, post_ref, share_ref,
    out_ref, tok_ref, state_in, state_out, normed, partial, wire, near_in, cross_out, cross_in, payload,
    st_send, st_recv, rs_send, rs_recv, xs_send, xs_recv, ag_send, ag_recv, own_sem,
):
    s = lax.axis_index("seq")
    e = lax.axis_index("exp")
    heads, hd, _ = map_ref.shape
    rows = res_ref.shape[0]
    dim = res_ref.shape[1]
    na = ne // 2
    a, c = e // 2, e % 2
    barrier = pltpu.get_barrier_semaphore()
    for i in range(1, ns):
        pl.semaphore_signal(barrier, inc=1, device_id=((s + i) % ns, e), device_id_type=MESH)
    for i in range(1, ne):
        pl.semaphore_signal(barrier, inc=1, device_id=(s, (e + i) % ne), device_id_type=MESH)
    pl.semaphore_wait(barrier, ns + ne - 2)

    def chain(h):
        return pltpu.make_async_remote_copy(
            src_ref=state_out.at[h], dst_ref=state_in.at[h], send_sem=st_send.at[h], recv_sem=st_recv.at[h],
            device_id=((s + 1) % ns, e), device_id_type=MESH,
        )

    @pl.when(s == 0)
    def _():
        state_in[...] = jnp.zeros_like(state_in)

    for h in range(heads):
        mh, ml = split(map_ref[h])

        @pl.when(s > 0)
        def _():
            chain(h).wait_recv()

        memory = state_in[h]
        state_out[h] = (mm(memory, mh) + mm(memory, ml) + write_ref[h]).astype(bf16)

        @pl.when(s < ns - 1)
        def _():
            chain(h).start()

    for h in range(heads):
        cols = slice(h * hd, (h + 1) * hd)
        memory = state_in[h]
        lh, ll = split(lift_ref[:, cols])
        core = lo_ref[:, cols] + (mm(lh, memory, NT) + mm(ll, memory, NT))
        mean = jnp.mean(core * core, axis=1, keepdims=True)
        valve = valve_ref[:, cols].astype(f32)
        normed[:, cols] = (core * lax.rsqrt(mean + epsilon) * gain_ref[...] * silu(valve)).astype(bf16)

    chunk = dim // 4
    for n in range(4):
        cols = slice(n * chunk, (n + 1) * chunk)
        product = mm(normed[...], w_ref[:, cols])
        for b in range(ne):
            partial[b, :, cols] = product[b * rows : (b + 1) * rows]
            wire[b, :, cols] = product[b * rows : (b + 1) * rows].astype(bf16)

    def near(i):
        there = (a + i) % na
        return pltpu.make_async_remote_copy(
            src_ref=wire.at[there * 2 + 1 - c], dst_ref=near_in.at[there], send_sem=rs_send.at[i], recv_sem=rs_recv.at[i],
            device_id=(s, a * 2 + 1 - c), device_id_type=MESH,
        )

    def cross(i):
        there = (a + i) % na
        return pltpu.make_async_remote_copy(
            src_ref=cross_out.at[i - 1], dst_ref=cross_in.at[i - 1], send_sem=xs_send.at[i - 1], recv_sem=xs_recv.at[i - 1],
            device_id=(s, there * 2 + c), device_id_type=MESH,
        )

    for i in range(na):
        near((i + 1) % na).start()
    for i in range(1, na):
        there = (a + i) % na
        near(i).wait_recv()
        cross_out[i - 1] = (partial[there * 2 + c] + near_in[there].astype(f32)).astype(bf16)
        cross(i).start()
    near(0).wait_recv()
    total = partial[e] + near_in[a].astype(f32)
    for i in range(1, na):
        cross(i).wait_recv()
        total = total + cross_in[i - 1].astype(f32)
    result = (res_ref[...].astype(f32) + total).astype(bf16)
    out_ref[...] = result
    mixed = result.astype(f32)
    tokens = (
        mixed * lax.rsqrt(jnp.mean(mixed * mixed, axis=1, keepdims=True) + epsilon) * post_ref[...]
    ).astype(bf16)
    sends = []
    if gather:
        payload[:, :dim] = tokens
        payload[:, dim:] = share_ref[...]
        nz = ns // 2
        z, y = s // 2, s % 2
        here = (z, y, a, c)
        half = dim // 2
        spans = (pl.ds(0, half), pl.ds(half, payload.shape[1] - half))

        def slot(p):
            return ((p[0] * 2 + p[1]) * na + p[2]) * 2 + p[3]

        own = pltpu.make_async_copy(payload, tok_ref.at[slot(here)], own_sem)
        own.start()

        def send(part, place, target, mine):
            index = slot(place)
            number = sum(1 for other, _ in sends if other == part)
            source = payload if mine else tok_ref.at[index]
            copy = pltpu.make_async_remote_copy(
                src_ref=source.at[:, spans[part]], dst_ref=tok_ref.at[index, :, spans[part]],
                send_sem=ag_send.at[part, number], recv_sem=ag_recv.at[part, index],
                device_id=(target[0] * 2 + target[1], target[2] * 2 + target[3]), device_id_type=MESH,
            )
            copy.start()
            sends.append((part, copy))

        def arrive(part, place):
            index = slot(place)
            pltpu.make_async_remote_copy(
                src_ref=payload.at[:, spans[part]], dst_ref=tok_ref.at[index, :, spans[part]],
                send_sem=ag_send.at[part, 0], recv_sem=ag_recv.at[part, index],
                device_id=(s, a * 2 + 1 - c), device_id_type=MESH,
            ).wait_recv()

        ypeer = (z, 1 - y, a, c)
        xpeer = (z, y, 1 - a, c)
        cpeer = (z, y, a, 1 - c)
        first, second = (ypeer, xpeer), (xpeer, ypeer)
        zs = [(z + i) % nz for i in range(nz)]
        back = [(z - i + nz) % nz for i in range(nz)]
        for i in range(1, nz):
            for part in (0, 1):
                send(part, here, (zs[i], y, a, c), True)
        for peers in (first, second, (cpeer, cpeer)):
            for part in (0, 1):
                send(part, here, peers[part], True)
        for i in range(1, nz):
            for part in (0, 1):
                place = (back[i], y, a, c)
                arrive(part, place)
                send(part, place, first[part], False)
                send(part, place, second[part], False)
                send(part, place, cpeer, False)
        for i in range(nz):
            for part in (0, 1):
                place = (back[i],) + first[part][1:]
                arrive(part, place)
                send(part, place, second[part], False)
                send(part, place, cpeer, False)
        for via in (0, 1):
            for i in range(nz):
                for part in (0, 1):
                    place = (back[i],) + second[part][1:]
                    if via:
                        place = (back[i], 1 - y, 1 - a, c)
                    arrive(part, place)
                    send(part, place, cpeer, False)
        for yy in (y, 1 - y):
            for aa in (a, 1 - a):
                for i in range(nz):
                    for part in (0, 1):
                        arrive(part, (back[i], yy, aa, 1 - c))
        own.wait()
    else:
        tok_ref[...] = tokens
    for _, copy in sends:
        copy.wait_send()
    for h in range(heads):
        @pl.when(s < ns - 1)
        def _():
            chain(h).wait_send()
    for i in range(na):
        near(i).wait_send()
    for i in range(1, na):
        cross(i).wait_send()


def mixer_call(ns, ne, gather, lo, lift, maps, writes, valve, gain, weight, residual, post, shares):
    heads, hd, _ = maps.shape
    tok_rows = lo.shape[0]
    rows, dim = residual.shape
    na = ne // 2
    width = dim + shares.shape[1]
    dma = pltpu.SemaphoreType.DMA
    tok_shape = (ns * ne, rows, width) if gather else (rows, dim)
    sent = (ns // 2 - 1) + 3 + 3 * (ns // 2 - 1) + 2 * (ns // 2) + 2 * (ns // 2)
    return pl.pallas_call(
        functools.partial(mixer_kernel, ns, ne, gather),
        in_specs=[VMEM] * 10,
        out_specs=[VMEM, ANY if gather else VMEM],
        out_shape=[jax.ShapeDtypeStruct((rows, dim), bf16), jax.ShapeDtypeStruct(tok_shape, bf16)],
        scratch_shapes=[
            pltpu.VMEM((heads, hd, hd), bf16), pltpu.VMEM((heads, hd, hd), bf16),
            pltpu.VMEM((tok_rows, heads * hd), bf16),
            pltpu.VMEM((ne, rows, dim), f32), pltpu.VMEM((ne, rows, dim), bf16),
            pltpu.VMEM((na, rows, dim), bf16),
            pltpu.VMEM((na - 1, rows, dim), bf16), pltpu.VMEM((na - 1, rows, dim), bf16),
            pltpu.VMEM((rows, width), bf16),
            dma((heads,)), dma((heads,)), dma((na,)), dma((na,)), dma((na - 1,)), dma((na - 1,)),
            dma((2, sent)), dma((2, ns * ne)), dma,
        ],
        compiler_params=pltpu.CompilerParams(
            collective_id=0, has_side_effects=True, vmem_limit_bytes=60 << 20
        ),
        name="mixer_tail",
    )(lo, lift, maps, writes, valve, gain, weight, residual, post, shares)


def expert_kernel(
    ns, ne, tok_ref, gate_hbm, up_hbm, down_hbm, sel_ref, out_ref, gate, up, down, xbuf, part, near_in, acc1,
    in_a, in_b, acc2a, acc2b, in2_a, in2_b, acc3, in3, w_sem, x_sem,
    n_send, n_recv, a_send, a_recv, b_send, b_recv, a2_send, a2_recv, b2_send, b2_recv, z_send, z_recv,
):
    s = lax.axis_index("seq")
    e = lax.axis_index("exp")
    nz = ns // 2
    z, y = s // 2, s % 2
    a, c = e // 2, e % 2
    own = gate.shape[0]
    rows, dim = out_ref.shape
    half = dim // 2
    lo, hi = pl.ds(0, half), pl.ds(half, half)
    yo, ao = 1 - y, 1 - a
    ypeer = (z * 2 + yo, e)
    xpeer = (s, ao * 2 + c)
    cpeer = (s, a * 2 + 1 - c)

    def load(i, kind):
        held, source = ((gate, gate_hbm), (up, up_hbm), (down, down_hbm))[kind]
        return pltpu.make_async_copy(source.at[i], held.at[i], w_sem.at[kind, i])

    def fetch(k, yy, place):
        return pltpu.make_async_copy(tok_ref.at[pl.ds((k * 2 + yy) * ne, ne)], xbuf.at[place], x_sem.at[place])

    def at(j):
        return (z + 1 + j) % nz

    fetch(at(0), yo, 0).start()
    for i in range(own):
        for kind in range(3):
            load(i, kind).start()
    barrier = pltpu.get_barrier_semaphore()
    peers = [ypeer, xpeer, cpeer] + [(((z + i) % nz) * 2 + y, e) for i in range(1, nz)]
    for peer in peers:
        pl.semaphore_signal(barrier, inc=1, device_id=peer, device_id_type=MESH)
    pl.semaphore_wait(barrier, len(peers))

    def copy(src, dst, ss, rs, to):
        return pltpu.make_async_remote_copy(
            src_ref=src, dst_ref=dst, send_sem=ss, recv_sem=rs, device_id=to, device_id_type=MESH
        )

    def near(k, yy, aa):
        f = (k * 2 + yy) * 2 + aa
        return copy(part.at[f * 2 + 1 - c], near_in.at[f], n_send.at[f], n_recv.at[f], cpeer)

    def step_a(k, yy):
        i = k * 2 + yy
        return copy(acc1.at[i * 2 + ao, :, lo], in_a.at[i], a_send.at[i], a_recv.at[i], xpeer)

    def step_b(k, aa):
        i = k * 2 + aa
        return copy(acc1.at[(k * 2 + yo) * 2 + aa, :, hi], in_b.at[i], b_send.at[i], b_recv.at[i], ypeer)

    def step_a2(k):
        return copy(acc2a.at[k * 2 + yo], in2_a.at[k], a2_send.at[k], a2_recv.at[k], ypeer)

    def step_b2(k):
        return copy(acc2b.at[k * 2 + ao], in2_b.at[k], b2_send.at[k], b2_recv.at[k], xpeer)

    def last(j):
        k = at(j)
        return copy(acc3.at[j], in3.at[j], z_send.at[j], z_recv.at[j], (k * 2 + y, e))

    def tile(k, yy, place, first):
        x = xbuf[place].reshape(ne * rows, xbuf.shape[-1])
        spread = x[:, dim:].astype(f32)
        inners = []
        for i in range(own):
            if first is not None:
                @pl.when(first)
                def _():
                    load(i, 0).wait()
                    load(i, 1).wait()
            share = jnp.sum(spread * sel_ref[i : i + 1, :], axis=1, keepdims=True)
            g = mm(x[:, :dim], gate[i])
            u = mm(x[:, :dim], up[i])
            inners.append((silu(g) * u * share).astype(bf16))
        if first is not None:
            @pl.when(first)
            def _():
                for i in range(own):
                    load(i, 2).wait()
        width = dim // 4
        base = (k * 2 + yy) * ne
        for n in range(4):
            cols = slice(n * width, (n + 1) * width)
            total = mm(inners[0], down[0, :, cols])
            for i in range(1, own):
                total = total + mm(inners[i], down[i, :, cols])
            for b in range(ne):
                part[base + b, :, cols] = total[b * rows : (b + 1) * rows].astype(bf16)
        near(k, yy, ao).start()
        near(k, yy, a).start()

    def second(k, yy, far):
        for aa, other in ((ao, True), (a, False)):
            f = (k * 2 + yy) * 2 + aa
            near(k, yy, aa).wait_recv()
            acc1[f] = (part[f * 2 + c].astype(f32) + near_in[f].astype(f32)).astype(bf16)
            if other:
                step_a(k, yy).start()
            if far:
                step_b(k, aa).start()

    def third(k):
        for far in (True, False):
            yy = yo if far else y
            aa = ao if far else a
            step_a(k, yy).wait_recv()
            i = k * 2 + yy
            acc2a[i] = (acc1[i * 2 + a, :, lo].astype(f32) + in_a[i].astype(f32)).astype(bf16)
            if far:
                step_a2(k).start()
            step_b(k, aa).wait_recv()
            i = k * 2 + aa
            acc2b[i] = (acc1[(k * 2 + y) * 2 + aa, :, hi].astype(f32) + in_b[i].astype(f32)).astype(bf16)
            if far:
                step_b2(k).start()

    def fourth(j):
        k = at(j)
        step_a2(k).wait_recv()
        acc3[j, :, lo] = (acc2a[k * 2 + y].astype(f32) + in2_a[k].astype(f32)).astype(bf16)
        step_b2(k).wait_recv()
        acc3[j, :, hi] = (acc2b[k * 2 + a].astype(f32) + in2_b[k].astype(f32)).astype(bf16)
        last(j).start()

    def lap(j, carry):
        k = at(j)
        fetch(k, y, 1).start()
        fetch(k, yo, 0).wait()
        tile(k, yo, 0, j == 0)

        @pl.when(j > 0)
        def _():
            second(at(j - 1), y, False)

        @pl.when(j > 1)
        def _():
            fourth(j - 2)

        @pl.when(j < nz - 1)
        def _():
            fetch(at(j + 1), yo, 0).start()

        fetch(k, y, 1).wait()
        tile(k, y, 1, None)
        second(k, yo, True)

        @pl.when(j > 0)
        def _():
            third(at(j - 1))

        return carry

    lax.fori_loop(0, nz, lap, 0)
    second(z, y, False)
    if nz > 1:
        fourth(nz - 2)
    third(z)
    step_a2(z).wait_recv()
    step_b2(z).wait_recv()
    left = acc2a[z * 2 + y].astype(f32) + in2_a[z].astype(f32)
    right = acc2b[z * 2 + a].astype(f32) + in2_b[z].astype(f32)
    for j in range(nz - 1):
        last(j).wait_recv()
        left = left + in3[j, :, lo].astype(f32)
        right = right + in3[j, :, hi].astype(f32)
    out_ref[:, lo] = left.astype(bf16)
    out_ref[:, hi] = right.astype(bf16)

    def drain(k, carry):
        for i in range(2):
            for aa in range(2):
                near(k, i, aa).wait_send()
            step_a(k, i).wait_send()
            step_b(k, i).wait_send()
        step_a2(k).wait_send()
        step_b2(k).wait_send()
        return carry

    lax.fori_loop(0, nz, drain, 0)
    for j in range(nz - 1):
        last(j).wait_send()


def expert_call(ns, ne, tokens, select, gate, up, down):
    rows, width = tokens.shape[1:]
    own, dim, ff = gate.shape
    nz = ns // 2
    half = dim // 2
    n = nz * 4
    dma = pltpu.SemaphoreType.DMA
    buf = lambda m, w: pltpu.VMEM((m, rows, w), bf16)
    counts = (n, 2 * nz, 2 * nz, nz, nz, nz - 1)
    return pl.pallas_call(
        functools.partial(expert_kernel, ns, ne),
        in_specs=[ANY, ANY, ANY, ANY, VMEM],
        out_specs=VMEM,
        out_shape=jax.ShapeDtypeStruct((rows, dim), bf16),
        scratch_shapes=[
            pltpu.VMEM(gate.shape, bf16), pltpu.VMEM(up.shape, bf16), pltpu.VMEM(down.shape, bf16),
            pltpu.VMEM((2, ne, rows, width), bf16),
            buf(2 * n, dim), buf(n, dim), buf(n, dim),
            buf(2 * nz, half), buf(2 * nz, half), buf(2 * nz, half), buf(2 * nz, half),
            buf(nz, half), buf(nz, half), buf(nz - 1, dim), buf(nz - 1, dim),
            dma((3, own)), dma((2,)),
        ] + [dma((m,)) for m in counts for _ in range(2)],
        compiler_params=pltpu.CompilerParams(
            collective_id=1, has_side_effects=True, vmem_limit_bytes=60 << 20
        ),
        name="experts_and_sum",
    )(tokens, gate, up, down, select)


def expert_mlp(arrived, expert_gate, expert_up, expert_down):
    gate_act = jnp.einsum(
        "secd,edf->secf", arrived, expert_gate, preferred_element_type=jnp.float32
    )
    up_act = jnp.einsum("secd,edf->secf", arrived, expert_up, preferred_element_type=jnp.float32)
    inner = (jax.nn.silu(gate_act) * up_act).astype(jnp.bfloat16)
    return jnp.einsum(
        "secf,efd->secd", inner, expert_down, preferred_element_type=jnp.float32
    ).astype(jnp.bfloat16)


def routed(moe_in, route_experts, route_weights, expert_gate, expert_up, expert_down):
    rows_dev, model_dim = moe_in.shape
    devices = lax.axis_size("seq") * lax.axis_size("exp")
    exp_dev = expert_gate.shape[0]
    expert_count = exp_dev * devices
    top_picks = route_experts.shape[1]
    capacity = 2 * ((rows_dev * top_picks + expert_count - 1) // expert_count)
    pick_count = rows_dev * top_picks
    linear_labels = route_experts.reshape(-1)
    expert_ids = jnp.arange(expert_count, dtype=jnp.int32)
    pick_table = (linear_labels[:, None] == expert_ids[None, :]).astype(jnp.bfloat16)
    row_index = lax.broadcasted_iota(jnp.int32, (pick_count, pick_count), 0)
    col_index = lax.broadcasted_iota(jnp.int32, (pick_count, pick_count), 1)
    earlier_picks = (row_index > col_index).astype(jnp.bfloat16)
    ranks = jnp.dot(earlier_picks, pick_table, preferred_element_type=jnp.float32)
    slot_index = jnp.take_along_axis(ranks, linear_labels[:, None], axis=1)[:, 0].astype(jnp.int32)
    position = linear_labels * capacity + slot_index
    source_row = (
        jnp.full((expert_count * capacity,), rows_dev, jnp.int32)
        .at[position]
        .set(jnp.arange(pick_count, dtype=jnp.int32) // top_picks)
    )
    padded_rows = jnp.concatenate([moe_in, jnp.zeros((1, model_dim), jnp.bfloat16)], axis=0)
    outgoing = padded_rows[source_row].reshape(devices, exp_dev, capacity, model_dim)
    finished = expert_mlp(
        lax.all_to_all(outgoing, ("seq", "exp"), split_axis=0, concat_axis=0, tiled=True),
        expert_gate,
        expert_up,
        expert_down,
    )
    returned = lax.all_to_all(finished, ("seq", "exp"), split_axis=0, concat_axis=0, tiled=True)
    flat_back = returned.reshape(expert_count * capacity, model_dim)
    picked = flat_back[position].reshape(rows_dev, top_picks, model_dim)
    shares = route_weights / jnp.sum(route_weights, axis=1, keepdims=True)
    expert_mixture = jnp.sum(picked.astype(jnp.float32) * shares[:, :, None], axis=1).astype(
        jnp.bfloat16
    )
    return expert_mixture


def body(
    query_proj,
    key_proj,
    value_proj,
    result_valve_maps,
    beta_logit,
    decay_logit,
    decay_rate,
    conv_query,
    conv_key,
    conv_value,
    norm_gain,
    output_weight,
    residual,
    post_gain,
    route_experts,
    route_weights,
    expert_gate,
    expert_up,
    expert_down,
):
    ns, ne = lax.axis_size("seq"), lax.axis_size("exp")
    tok_rows = query_proj.shape[0]
    head_dim = norm_gain.shape[0]
    rim_width = conv_query.shape[0] - 1
    edge = jnp.concatenate(
        [
            query_proj[tok_rows - rim_width :],
            key_proj[tok_rows - rim_width :],
            value_proj[tok_rows - rim_width :],
        ],
        axis=1,
    )
    leading = shifted(edge, "seq", 1).astype(jnp.float32)
    beta = jax.nn.sigmoid(beta_logit)
    log_decay = -decay_rate[None, :] * jax.nn.softplus(decay_logit)
    lo, lift, maps, writes = local_terms(
        query_proj, key_proj, value_proj, leading, conv_query, conv_key, conv_value, beta, log_decay, head_dim
    )
    rows, dim = residual.shape
    own = expert_gate.shape[0]
    experts = own * ns * ne
    lanes = -(-experts // 128) * 128
    dense = ne == 4 and ns % 2 == 0 and ns * ne * rows * dim * 2 <= 8 << 20 and own * ff_bytes(expert_gate) <= 12 << 20
    shares = route_weights / jnp.sum(route_weights, axis=1, keepdims=True)
    lane = jnp.arange(lanes, dtype=jnp.int32)
    table = jnp.sum(
        jnp.where(route_experts[:, :, None] == lane[None, None, :], shares[:, :, None], 0.0), axis=1
    ).astype(bf16)
    mixer_out, tokens = mixer_call(
        ns, ne, dense, lo, lift, maps, writes, result_valve_maps, norm_gain[None, :], output_weight, residual,
        post_gain[None, :], table,
    )
    if not dense:
        return mixer_out, routed(tokens, route_experts, route_weights, expert_gate, expert_up, expert_down)
    place = lax.axis_index("seq") * ne + lax.axis_index("exp")
    mine = place * own + jnp.arange(own, dtype=jnp.int32)
    select = (lane[None, :] == mine[:, None]).astype(f32)
    return mixer_out, expert_call(ns, ne, tokens, select, expert_gate, expert_up, expert_down)


def ff_bytes(weight):
    return 3 * weight.shape[1] * weight.shape[2] * 2


def solution(mesh):
    in_specs = (
        P("seq", "exp"),
        P("seq", "exp"),
        P("seq", "exp"),
        P("seq", "exp"),
        P("seq", "exp"),
        P("seq", "exp"),
        P("exp"),
        P(None, "exp"),
        P(None, "exp"),
        P(None, "exp"),
        P(),
        P("exp", None),
        P(("seq", "exp"), None),
        P(),
        P(("seq", "exp"), None),
        P(("seq", "exp"), None),
        P(("seq", "exp"), None, None),
        P(("seq", "exp"), None, None),
        P(("seq", "exp"), None, None),
    )
    out_specs = (P(("seq", "exp"), None), P(("seq", "exp"), None))
    return jax.shard_map(body, mesh=mesh, in_specs=in_specs, out_specs=out_specs, check_vma=False)
```

```python
import functools

import jax
import jax.numpy as jnp
from jax import lax
from jax.experimental import pallas as pl
from jax.experimental.pallas import tpu as pltpu
from jax.sharding import PartitionSpec as P

epsilon = 1e-06
f32 = jnp.float32
bf16 = jnp.bfloat16
MESH = pl.DeviceIdType.MESH
NN = (((1,), (0,)), ((), ()))
NT = (((1,), (1,)), ((), ()))
TN = (((0,), (0,)), ((), ()))
VMEM = pl.BlockSpec(memory_space=pltpu.VMEM)
ANY = pl.BlockSpec(memory_space=pl.ANY)


def shifted(value, axis, steps):
    count = lax.axis_size(axis)
    leading, last = (max(0, -steps), min(count, count - steps))
    return lax.ppermute(value, axis, [(source, source + steps) for source in range(leading, last)])


def silu(x):
    return x / (1.0 + jnp.exp(-x))


def mm(a, b, dims=NN):
    return lax.dot_general(a, b, dims, preferred_element_type=f32)


def split(x):
    high = x.astype(bf16)
    return high, (x - high.astype(f32)).astype(bf16)


def dot3(a, b, dims=NN):
    ah, al = split(a)
    bh, bl = split(b)
    return mm(ah, bh, dims) + (mm(ah, bl, dims) + mm(al, bh, dims))


def conv_act(x_ref, halo_ref, w_ref):
    taps = w_ref.shape[0]
    rows = x_ref.shape[0]
    top = halo_ref.shape[0]
    padded = jnp.concatenate([halo_ref[...].astype(f32), x_ref[...].astype(f32)], axis=0)
    total = w_ref[taps - 1 : taps, :] * padded[top : top + rows]
    for j in range(taps - 1):
        start = top - (taps - 1) + j
        total = total + w_ref[j : j + 1, :] * padded[start : start + rows]
    return silu(total)


def local_kernel(
    hd, q_ref, k_ref, v_ref, hq_ref, hk_ref, hv_ref, wq_ref, wk_ref, wv_ref,
    logit_ref, decay_ref, rate_ref, lo_ref, lift_ref, map_ref, write_ref, coup, inv, score,
):
    rows = q_ref.shape[0]
    key_heads = q_ref.shape[1] // hd
    heads = v_ref.shape[1] // hd
    per = heads // key_heads
    q = conv_act(q_ref, hq_ref, wq_ref)
    k = conv_act(k_ref, hk_ref, wk_ref)
    v = conv_act(v_ref, hv_ref, wv_ref)
    ri = lax.broadcasted_iota(jnp.int32, (rows, rows), 0)
    ci = lax.broadcasted_iota(jnp.int32, (rows, rows), 1)
    apart = ri ^ ci
    low = ri >= ci
    strict = ri > ci
    group = pl.program_id(0)

    def chosen(ref):
        picked = ref[:, :heads]
        for g in range(1, ref.shape[1] // heads):
            picked = jnp.where(group == g, ref[:, g * heads : (g + 1) * heads], picked)
        return picked

    logit, decay_in, rate = chosen(logit_ref), chosen(decay_ref), chosen(rate_ref)
    beta_all = 1.0 / (1.0 + jnp.exp(-logit))
    log_decay = -rate * (jnp.maximum(decay_in, 0.0) + jnp.log1p(jnp.exp(-jnp.abs(decay_in))))
    bounded = jnp.maximum(log_decay, -110.0)
    whole = jnp.floor(bounded)
    fraction = bounded - whole
    f_high, f_rest = fraction.astype(bf16), fraction - fraction.astype(bf16).astype(f32)
    f_mid, f_low = split(f_rest)
    lower = jnp.where(low, 1.0, 0.0).astype(bf16)
    upper = jnp.where(ri <= ci, 1.0, 0.0).astype(bf16)
    whole = whole.astype(bf16)
    cum_w = mm(lower, whole)
    cum_f = mm(lower, f_high) + (mm(lower, f_mid) + mm(lower, f_low))
    cumt_w = mm(whole, upper, TN)
    cumt_f = mm(f_high, upper, TN) + (mm(f_mid, upper, TN) + mm(f_low, upper, TN))
    qs, ks = [], []
    for a in range(key_heads):
        ka = k[:, a * hd : (a + 1) * hd]
        ka = ka * lax.rsqrt(jnp.sum(ka * ka, axis=1, keepdims=True) + epsilon)
        qa = q[:, a * hd : (a + 1) * hd]
        qs.append(qa)
        ks.append(ka)
        kk = dot3(ka, ka, NT)
        qk = dot3(qa, ka, NT)
        for h in range(a * per, (a + 1) * per):
            spread = (cum_w[:, h : h + 1] - cumt_w[h : h + 1, :]) + (cum_f[:, h : h + 1] - cumt_f[h : h + 1, :])
            decay = jnp.where(low, jnp.exp(jnp.where(low, spread, 0.0)), 0.0)
            coupling = jnp.where(strict, beta_all[:, h : h + 1] * kk * decay, 0.0)
            coup[h] = coupling
            score[h] = qk * decay
            inv[h] = jnp.where(ri == ci, 1.0, 0.0) - jnp.where(apart == 1, coupling, 0.0)

    half = rows // 2
    near_bits = apart[:half, :half]

    def level(step, carry):
        near = lax.shift_right_logical(near_bits, jnp.full_like(near_bits, step)) == 1
        for h in range(heads):
            for part in (slice(0, half), slice(half, rows)):
                x = inv[h, part, part]
                c = jnp.where(near, coup[h, part, part], 0.0)
                inv[h, part, part] = x - dot3(x, dot3(c, x))
        return carry

    lax.fori_loop(1, (half - 1).bit_length(), level, 0)
    for h in range(heads):
        inv[h, half:, :half] = -dot3(inv[h, half:, half:], dot3(coup[h, half:, :half], inv[h, :half, :half]))
    eye = jnp.where(
        lax.broadcasted_iota(jnp.int32, (hd, hd), 0) == lax.broadcasted_iota(jnp.int32, (hd, hd), 1), 1.0, 0.0
    )
    for h in range(heads):
        growth = jnp.exp(cum_w[:, h : h + 1] + cum_f[:, h : h + 1])
        last_w = cum_w[rows - 1 : rows, h : h + 1]
        last_f = cum_f[rows - 1 : rows, h : h + 1]
        remain = jnp.exp((last_w - cum_w[:, h : h + 1]) + (last_f - cum_f[:, h : h + 1]))
        beta = beta_all[:, h : h + 1]
        qa, ka = qs[h // per], ks[h // per]
        stacked = jnp.concatenate([beta * v[:, h * hd : (h + 1) * hd], (beta * growth) * ka], axis=1)
        solved = dot3(inv[h], stacked)
        mixed = dot3(score[h], solved)
        lo_ref[:, h * hd : (h + 1) * hd] = mixed[:, :hd]
        lift_ref[:, h * hd : (h + 1) * hd] = growth * qa - mixed[:, hd:]
        ends = dot3(solved, ka * remain, TN)
        write_ref[h] = ends[:hd]
        map_ref[h] = jnp.exp(last_w + last_f) * eye - ends[hd:]


def local_terms(q, k, v, halo, wq, wk, wv, logit, decay, rate, hd):
    rows, kc = q.shape
    vc = v.shape[1]
    heads = vc // hd
    groups = 2 if (kc // hd) % 2 == 0 and 2 * kc % vc == 0 else 1
    gh = heads // groups
    kw, vw = kc // groups, vc // groups
    taps, top = wq.shape[0], halo.shape[0]
    whole = lambda r: pl.BlockSpec((r, heads), lambda g: (0, 0))
    col = lambda r, w: pl.BlockSpec((r, w), lambda g: (0, g))
    mats = pl.BlockSpec((gh, hd, hd), lambda g: (g, 0, 0))
    return pl.pallas_call(
        functools.partial(local_kernel, hd),
        grid=(groups,),
        in_specs=[
            col(rows, kw), col(rows, kw), col(rows, vw),
            pl.BlockSpec((top, kw), lambda g: (0, g)),
            pl.BlockSpec((top, kw), lambda g: (0, kc // kw + g)),
            pl.BlockSpec((top, vw), lambda g: (0, 2 * kc // vw + g)),
            col(taps, kw), col(taps, kw), col(taps, vw),
            whole(rows), whole(rows), whole(1),
        ],
        out_specs=[col(rows, vw), col(rows, vw), mats, mats],
        out_shape=[
            jax.ShapeDtypeStruct((rows, vc), f32),
            jax.ShapeDtypeStruct((rows, vc), f32),
            jax.ShapeDtypeStruct((heads, hd, hd), f32),
            jax.ShapeDtypeStruct((heads, hd, hd), f32),
        ],
        scratch_shapes=[pltpu.VMEM((gh, rows, rows), f32)] * 3,
        compiler_params=pltpu.CompilerParams(vmem_limit_bytes=60 << 20),
        name="block_terms",
    )(q, k, v, halo, halo, halo, wq, wk, wv, logit, decay, rate)


def mixer_kernel(
    ns, ne, gather, lo_ref, lift_ref, map_ref, write_ref, valve_ref, gain_ref, w_ref, res_ref, post_ref, pick_ref, weight_ref,
    out_ref, tok_ref, state_in, state_out, normed, partial, wire, near_in, cross_out, cross_in,
    st_send, st_recv, rs_send, rs_recv, xs_send, xs_recv,
):
    s = lax.axis_index("seq")
    e = lax.axis_index("exp")
    heads, hd, _ = map_ref.shape
    rows = res_ref.shape[0]
    dim = res_ref.shape[1]
    na = ne // 2
    a, c = e // 2, e % 2
    barrier = pltpu.get_barrier_semaphore()
    for i in range(1, ns):
        pl.semaphore_signal(barrier, inc=1, device_id=((s + i) % ns, e), device_id_type=MESH)
    for i in range(1, ne):
        pl.semaphore_signal(barrier, inc=1, device_id=(s, (e + i) % ne), device_id_type=MESH)
    pl.semaphore_wait(barrier, ns + ne - 2)

    def chain(h):
        return pltpu.make_async_remote_copy(
            src_ref=state_out.at[h], dst_ref=state_in.at[h], send_sem=st_send.at[h], recv_sem=st_recv.at[h],
            device_id=((s + 1) % ns, e), device_id_type=MESH,
        )

    @pl.when(s == 0)
    def _():
        state_in[...] = jnp.zeros_like(state_in)

    if gather:
        shares = weight_ref[...] / jnp.sum(weight_ref[...], axis=1, keepdims=True)
        lane = lax.broadcasted_iota(jnp.int32, (rows, tok_ref.shape[1] - dim), 1)
        table = jnp.zeros(lane.shape, f32)
        for pick in range(pick_ref.shape[1]):
            table = table + jnp.where(pick_ref[:, pick : pick + 1] == lane, shares[:, pick : pick + 1], 0.0)
        tok_ref[:, dim:] = table.astype(bf16)

    for h in range(heads):
        mh, ml = split(map_ref[h])

        @pl.when(s > 0)
        def _():
            chain(h).wait_recv()

        memory = state_in[h]
        state_out[h] = (mm(memory, mh) + mm(memory, ml) + write_ref[h]).astype(bf16)

        @pl.when(s < ns - 1)
        def _():
            chain(h).start()

    for h in range(heads):
        cols = slice(h * hd, (h + 1) * hd)
        memory = state_in[h]
        lh, ll = split(lift_ref[:, cols])
        core = lo_ref[:, cols] + (mm(lh, memory, NT) + mm(ll, memory, NT))
        mean = jnp.mean(core * core, axis=1, keepdims=True)
        valve = valve_ref[:, cols].astype(f32)
        normed[:, cols] = (core * lax.rsqrt(mean + epsilon) * gain_ref[...] * silu(valve)).astype(bf16)

    chunk = dim // 4
    for n in range(4):
        cols = slice(n * chunk, (n + 1) * chunk)
        product = mm(normed[...], w_ref[:, cols])
        for b in range(ne):
            partial[b, :, cols] = product[b * rows : (b + 1) * rows]
            wire[b, :, cols] = product[b * rows : (b + 1) * rows].astype(bf16)

    def near(i):
        there = (a + i) % na
        return pltpu.make_async_remote_copy(
            src_ref=wire.at[there * 2 + 1 - c], dst_ref=near_in.at[there], send_sem=rs_send.at[i], recv_sem=rs_recv.at[i],
            device_id=(s, a * 2 + 1 - c), device_id_type=MESH,
        )

    def cross(i):
        there = (a + i) % na
        return pltpu.make_async_remote_copy(
            src_ref=cross_out.at[i - 1], dst_ref=cross_in.at[i - 1], send_sem=xs_send.at[i - 1], recv_sem=xs_recv.at[i - 1],
            device_id=(s, there * 2 + c), device_id_type=MESH,
        )

    for i in range(na):
        near((i + 1) % na).start()
    for i in range(1, na):
        there = (a + i) % na
        near(i).wait_recv()
        cross_out[i - 1] = (partial[there * 2 + c] + near_in[there].astype(f32)).astype(bf16)
        cross(i).start()
    near(0).wait_recv()
    total = partial[e] + near_in[a].astype(f32)
    for i in range(1, na):
        cross(i).wait_recv()
        total = total + cross_in[i - 1].astype(f32)
    result = (res_ref[...].astype(f32) + total).astype(bf16)
    out_ref[...] = result
    mixed = result.astype(f32)
    tokens = (
        mixed * lax.rsqrt(jnp.mean(mixed * mixed, axis=1, keepdims=True) + epsilon) * post_ref[...]
    ).astype(bf16)
    tok_ref[:, :dim] = tokens
    for h in range(heads):
        @pl.when(s < ns - 1)
        def _():
            chain(h).wait_send()
    for i in range(na):
        near(i).wait_send()
    for i in range(1, na):
        cross(i).wait_send()


def mixer_call(ns, ne, gather, lo, lift, maps, writes, valve, gain, weight, residual, post, picks, pick_weights, lanes):
    heads, hd, _ = maps.shape
    tok_rows = lo.shape[0]
    rows, dim = residual.shape
    na = ne // 2
    width = dim + lanes if gather else dim
    dma = pltpu.SemaphoreType.DMA
    return pl.pallas_call(
        functools.partial(mixer_kernel, ns, ne, gather),
        in_specs=[VMEM] * 11,
        out_specs=[VMEM, VMEM],
        out_shape=[jax.ShapeDtypeStruct((rows, dim), bf16), jax.ShapeDtypeStruct((rows, width), bf16)],
        scratch_shapes=[
            pltpu.VMEM((heads, hd, hd), bf16), pltpu.VMEM((heads, hd, hd), bf16),
            pltpu.VMEM((tok_rows, heads * hd), bf16),
            pltpu.VMEM((ne, rows, dim), f32), pltpu.VMEM((ne, rows, dim), bf16),
            pltpu.VMEM((na, rows, dim), bf16),
            pltpu.VMEM((na - 1, rows, dim), bf16), pltpu.VMEM((na - 1, rows, dim), bf16),
            dma((heads,)), dma((heads,)), dma((na,)), dma((na,)), dma((na - 1,)), dma((na - 1,)),
        ],
        compiler_params=pltpu.CompilerParams(
            collective_id=0, has_side_effects=True, vmem_limit_bytes=60 << 20
        ),
        name="mixer_tail",
    )(lo, lift, maps, writes, valve, gain, weight, residual, post, picks, pick_weights)


def expert_kernel(
    ns, ne, payload, gate_hbm, up_hbm, down_hbm, out_ref, tok_ref, gate, up, down, xbuf, part, near_in, acc1,
    in_a, in_b, acc2a, acc2b, in2_a, in2_b, acc3, in3, w_sem, x_sem,
    g_send, gz_send, g_recv, own_sem,
    n_send, n_recv, a_send, a_recv, b_send, b_recv, a2_send, a2_recv, b2_send, b2_recv, z_send, z_recv,
):
    s = lax.axis_index("seq")
    e = lax.axis_index("exp")
    nz = ns // 2
    z, y = s // 2, s % 2
    a, c = e // 2, e % 2
    own = gate.shape[0]
    rows, dim = out_ref.shape
    half = dim // 2
    lo, hi = pl.ds(0, half), pl.ds(half, half)
    yo, ao = 1 - y, 1 - a
    ypeer = (z * 2 + yo, e)
    xpeer = (s, ao * 2 + c)
    cpeer = (s, a * 2 + 1 - c)

    def load(i, kind):
        held, source = ((gate, gate_hbm), (up, up_hbm), (down, down_hbm))[kind]
        return pltpu.make_async_copy(source.at[i], held.at[i], w_sem.at[kind, i])

    def fetch(k, yy, place):
        return pltpu.make_async_copy(tok_ref.at[pl.ds((k * 2 + yy) * ne, ne)], xbuf.at[place], x_sem.at[place])

    def at(j):
        return (z - j + nz) % nz

    for i in range(own):
        for kind in range(3):
            load(i, kind).start()
    barrier = pltpu.get_barrier_semaphore()
    peers = [ypeer, xpeer, cpeer] + [(((z + i) % nz) * 2 + y, e) for i in range(1, nz)]
    for peer in peers:
        pl.semaphore_signal(barrier, inc=1, device_id=peer, device_id_type=MESH)
    pl.semaphore_wait(barrier, len(peers))

    def copy(src, dst, ss, rs, to):
        return pltpu.make_async_remote_copy(
            src_ref=src, dst_ref=dst, send_sem=ss, recv_sem=rs, device_id=to, device_id_type=MESH
        )

    def near(k, yy, aa):
        f = (k * 2 + yy) * 2 + aa
        return copy(part.at[f * 2 + 1 - c], near_in.at[f], n_send.at[f], n_recv.at[f], cpeer)

    def step_a(k, yy):
        i = k * 2 + yy
        return copy(acc1.at[i * 2 + ao, :, lo], in_a.at[i], a_send.at[i], a_recv.at[i], xpeer)

    def step_b(k, aa):
        i = k * 2 + aa
        return copy(acc1.at[(k * 2 + yo) * 2 + aa, :, hi], in_b.at[i], b_send.at[i], b_recv.at[i], ypeer)

    def step_a2(k):
        return copy(acc2a.at[k * 2 + yo], in2_a.at[k], a2_send.at[k], a2_recv.at[k], ypeer)

    def step_b2(k):
        return copy(acc2b.at[k * 2 + ao], in2_b.at[k], b2_send.at[k], b2_recv.at[k], xpeer)

    def last(j):
        k = at(j)
        return copy(acc3.at[j - 1], in3.at[j - 1], z_send.at[j - 1], z_recv.at[j - 1], (k * 2 + y, e))

    cut = (pl.ds(0, half), pl.ds(half, payload.shape[1] - half))
    routes = (((yo, a), (y, ao)), ((y, ao), (yo, a)))

    def slot(k, yy, aa, cc):
        return ((k * 2 + yy) * 2 + aa) * 2 + cc

    def pass_on(half_at, j, number, place, target, mine=False):
        source = payload.at[:, cut[half_at]] if mine else tok_ref.at[place, :, cut[half_at]]
        return copy(
            source, tok_ref.at[place, :, cut[half_at]], g_send.at[half_at, j, number], g_recv.at[half_at, place], target
        )

    def hop(half_at, step):
        yy, aa = routes[half_at][step]
        return (z * 2 + yy, aa * 2 + c)

    def arrive(half_at, place):
        pass_on(half_at, 0, 0, place, cpeer).wait_recv()

    def stage(j, number, mine=False):
        for half_at in (0, 1):
            first_place, second_place = routes[half_at]
            yy, aa = ((y, a), first_place, second_place, (yo, ao))[number]
            place = slot(at(j), yy, aa, c)
            if not mine:
                arrive(half_at, place)
            if number == 0:
                pass_on(half_at, j, 0, place, hop(half_at, 0), mine).start()
            if number < 2:
                pass_on(half_at, j, 1 + number, place, hop(half_at, 1), mine).start()
            pass_on(half_at, j, 3 + number, place, cpeer, mine).start()

    def ended(j):
        for number in range(7):
            for half_at in (0, 1):
                pass_on(half_at, j, number, 0, cpeer).wait_send()

    def landed(j):
        for yy in (y, yo):
            for aa in (a, ao):
                for half_at in (0, 1):
                    arrive(half_at, slot(at(j), yy, aa, 1 - c))

    def give(half_at, j):
        place = slot(z, y, a, c)
        return copy(
            payload.at[:, cut[half_at]], tok_ref.at[place, :, cut[half_at]], gz_send.at[half_at, j - 1],
            g_recv.at[half_at, place], (((z + j) % nz) * 2 + y, e),
        )

    mine_copy = pltpu.make_async_copy(payload, tok_ref.at[slot(z, y, a, c)], own_sem)
    mine_copy.start()
    stage(0, 0, True)
    for j in range(1, nz):
        for half_at in (0, 1):
            give(half_at, j).start()
    for number in (1, 2, 3):
        stage(0, number)
    if nz > 1:
        stage(1, 0)
    landed(0)
    mine_copy.wait()

    lane = lax.broadcasted_iota(jnp.int32, (ne * rows, xbuf.shape[-1] - dim), 1)

    def tile(k, yy, place, first, between):
        x = xbuf[place].reshape(ne * rows, xbuf.shape[-1])
        spread = x[:, dim:].astype(f32)
        inners = []
        for i in range(own):
            if first is not None:
                @pl.when(first)
                def _():
                    load(i, 0).wait()
                    load(i, 1).wait()
            share = jnp.sum(jnp.where(lane == (s * ne + e) * own + i, spread, 0.0), axis=1, keepdims=True)
            g = mm(x[:, :dim], gate[i])
            u = mm(x[:, :dim], up[i])
            inners.append((silu(g) * u * share).astype(bf16))
        between()
        if first is not None:
            @pl.when(first)
            def _():
                for i in range(own):
                    load(i, 2).wait()
        width = dim // 4
        base = (k * 2 + yy) * ne
        for n in range(4):
            cols = slice(n * width, (n + 1) * width)
            total = mm(inners[0], down[0, :, cols])
            for i in range(1, own):
                total = total + mm(inners[i], down[i, :, cols])
            for b in range(ne):
                part[base + b, :, cols] = total[b * rows : (b + 1) * rows].astype(bf16)
        near(k, yy, ao).start()
        near(k, yy, a).start()

    def second(k, yy, far):
        for aa, other in ((ao, True), (a, False)):
            f = (k * 2 + yy) * 2 + aa
            near(k, yy, aa).wait_recv()
            acc1[f] = (part[f * 2 + c].astype(f32) + near_in[f].astype(f32)).astype(bf16)
            if other:
                step_a(k, yy).start()
            if far:
                step_b(k, aa).start()

    def third(k):
        for far in (True, False):
            yy = yo if far else y
            aa = ao if far else a
            step_a(k, yy).wait_recv()
            i = k * 2 + yy
            acc2a[i] = (acc1[i * 2 + a, :, lo].astype(f32) + in_a[i].astype(f32)).astype(bf16)
            if far:
                step_a2(k).start()
            step_b(k, aa).wait_recv()
            i = k * 2 + aa
            acc2b[i] = (acc1[(k * 2 + y) * 2 + aa, :, hi].astype(f32) + in_b[i].astype(f32)).astype(bf16)
            if far:
                step_b2(k).start()

    def fourth(j):
        k = at(j)
        step_a2(k).wait_recv()
        acc3[j - 1, :, lo] = (acc2a[k * 2 + y].astype(f32) + in2_a[k].astype(f32)).astype(bf16)
        step_b2(k).wait_recv()
        acc3[j - 1, :, hi] = (acc2b[k * 2 + a].astype(f32) + in2_b[k].astype(f32)).astype(bf16)
        last(j).start()

    def lap(j, carry):
        k = at(j)
        more = j < nz - 1
        fetch(k, yo, 0).start()
        fetch(k, y, 1).start()

        def after(number):
            @pl.when(more)
            def _():
                stage(j + 1, number)

        fetch(k, yo, 0).wait()
        tile(k, yo, 0, j == 0, lambda: after(1))

        @pl.when(j > 0)
        def _():
            second(at(j - 1), y, False)

        @pl.when(j > 2)
        def _():
            fourth(j - 2)

        after(2)
        fetch(k, y, 1).wait()
        tile(k, y, 1, None, lambda: after(3))

        @pl.when(j < nz - 2)
        def _():
            stage(j + 2, 0)

        second(k, yo, True)

        @pl.when(j > 0)
        def _():
            third(at(j - 1))

        @pl.when(more)
        def _():
            landed(j + 1)

        return carry

    lax.fori_loop(0, nz, lap, 0)
    second(at(nz - 1), y, False)
    if nz > 2:
        fourth(nz - 2)
    third(at(nz - 1))
    if nz > 1:
        fourth(nz - 1)
    step_a2(z).wait_recv()
    step_b2(z).wait_recv()
    left = acc2a[z * 2 + y].astype(f32) + in2_a[z].astype(f32)
    right = acc2b[z * 2 + a].astype(f32) + in2_b[z].astype(f32)
    for j in range(1, nz):
        last(j).wait_recv()
        left = left + in3[j - 1, :, lo].astype(f32)
        right = right + in3[j - 1, :, hi].astype(f32)
    out_ref[:, lo] = left.astype(bf16)
    out_ref[:, hi] = right.astype(bf16)

    def drain(k, carry):
        for i in range(2):
            for aa in range(2):
                near(k, i, aa).wait_send()
            step_a(k, i).wait_send()
            step_b(k, i).wait_send()
        step_a2(k).wait_send()
        step_b2(k).wait_send()
        ended(k)
        return carry

    lax.fori_loop(0, nz, drain, 0)
    for j in range(1, nz):
        last(j).wait_send()
        for half_at in (0, 1):
            give(half_at, j).wait_send()


def expert_call(ns, ne, tokens, gate, up, down):
    rows, width = tokens.shape
    own, dim, ff = gate.shape
    nz = ns // 2
    half = dim // 2
    n = nz * 4
    dma = pltpu.SemaphoreType.DMA
    buf = lambda m, w: pltpu.VMEM((m, rows, w), bf16)
    counts = (n, 2 * nz, 2 * nz, nz, nz, nz - 1)
    return pl.pallas_call(
        functools.partial(expert_kernel, ns, ne),
        in_specs=[VMEM, ANY, ANY, ANY],
        out_specs=[VMEM, ANY],
        out_shape=[
            jax.ShapeDtypeStruct((rows, dim), bf16),
            jax.ShapeDtypeStruct((ns * ne, rows, width), bf16),
        ],
        scratch_shapes=[
            pltpu.VMEM(gate.shape, bf16), pltpu.VMEM(up.shape, bf16), pltpu.VMEM(down.shape, bf16),
            pltpu.VMEM((2, ne, rows, width), bf16),
            buf(2 * n, dim), buf(n, dim), buf(n, dim),
            buf(2 * nz, half), buf(2 * nz, half), buf(2 * nz, half), buf(2 * nz, half),
            buf(nz, half), buf(nz, half), buf(nz - 1, dim), buf(nz - 1, dim),
            dma((3, own)), dma((2,)),
            dma((2, nz, 7)), dma((2, nz - 1)), dma((2, ns * ne)), dma,
        ] + [dma((m,)) for m in counts for _ in range(2)],
        compiler_params=pltpu.CompilerParams(
            collective_id=1, has_side_effects=True, vmem_limit_bytes=60 << 20
        ),
        name="experts_and_sum",
    )(tokens, gate, up, down)[0]


def expert_mlp(arrived, expert_gate, expert_up, expert_down):
    gate_act = jnp.einsum(
        "secd,edf->secf", arrived, expert_gate, preferred_element_type=jnp.float32
    )
    up_act = jnp.einsum("secd,edf->secf", arrived, expert_up, preferred_element_type=jnp.float32)
    inner = (jax.nn.silu(gate_act) * up_act).astype(jnp.bfloat16)
    return jnp.einsum(
        "secf,efd->secd", inner, expert_down, preferred_element_type=jnp.float32
    ).astype(jnp.bfloat16)


def routed(moe_in, route_experts, route_weights, expert_gate, expert_up, expert_down):
    rows_dev, model_dim = moe_in.shape
    devices = lax.axis_size("seq") * lax.axis_size("exp")
    exp_dev = expert_gate.shape[0]
    expert_count = exp_dev * devices
    top_picks = route_experts.shape[1]
    capacity = 2 * ((rows_dev * top_picks + expert_count - 1) // expert_count)
    pick_count = rows_dev * top_picks
    linear_labels = route_experts.reshape(-1)
    expert_ids = jnp.arange(expert_count, dtype=jnp.int32)
    pick_table = (linear_labels[:, None] == expert_ids[None, :]).astype(jnp.bfloat16)
    row_index = lax.broadcasted_iota(jnp.int32, (pick_count, pick_count), 0)
    col_index = lax.broadcasted_iota(jnp.int32, (pick_count, pick_count), 1)
    earlier_picks = (row_index > col_index).astype(jnp.bfloat16)
    ranks = jnp.dot(earlier_picks, pick_table, preferred_element_type=jnp.float32)
    slot_index = jnp.take_along_axis(ranks, linear_labels[:, None], axis=1)[:, 0].astype(jnp.int32)
    position = linear_labels * capacity + slot_index
    source_row = (
        jnp.full((expert_count * capacity,), rows_dev, jnp.int32)
        .at[position]
        .set(jnp.arange(pick_count, dtype=jnp.int32) // top_picks)
    )
    padded_rows = jnp.concatenate([moe_in, jnp.zeros((1, model_dim), jnp.bfloat16)], axis=0)
    outgoing = padded_rows[source_row].reshape(devices, exp_dev, capacity, model_dim)
    finished = expert_mlp(
        lax.all_to_all(outgoing, ("seq", "exp"), split_axis=0, concat_axis=0, tiled=True),
        expert_gate,
        expert_up,
        expert_down,
    )
    returned = lax.all_to_all(finished, ("seq", "exp"), split_axis=0, concat_axis=0, tiled=True)
    flat_back = returned.reshape(expert_count * capacity, model_dim)
    picked = flat_back[position].reshape(rows_dev, top_picks, model_dim)
    shares = route_weights / jnp.sum(route_weights, axis=1, keepdims=True)
    expert_mixture = jnp.sum(picked.astype(jnp.float32) * shares[:, :, None], axis=1).astype(
        jnp.bfloat16
    )
    return expert_mixture


def body(
    query_proj,
    key_proj,
    value_proj,
    result_valve_maps,
    beta_logit,
    decay_logit,
    decay_rate,
    conv_query,
    conv_key,
    conv_value,
    norm_gain,
    output_weight,
    residual,
    post_gain,
    route_experts,
    route_weights,
    expert_gate,
    expert_up,
    expert_down,
):
    ns, ne = lax.axis_size("seq"), lax.axis_size("exp")
    tok_rows = query_proj.shape[0]
    head_dim = norm_gain.shape[0]
    rim_width = -(-(conv_query.shape[0] - 1) // 8) * 8
    edge = jnp.concatenate(
        [
            query_proj[tok_rows - rim_width :],
            key_proj[tok_rows - rim_width :],
            value_proj[tok_rows - rim_width :],
        ],
        axis=1,
    )
    leading = shifted(edge, "seq", 1)
    lo, lift, maps, writes = local_terms(
        query_proj, key_proj, value_proj, leading, conv_query, conv_key, conv_value, beta_logit, decay_logit,
        decay_rate[None, :], head_dim,
    )
    rows, dim = residual.shape
    own = expert_gate.shape[0]
    experts = own * ns * ne
    lanes = -(-experts // 128) * 128
    dense = ne == 4 and ns % 2 == 0 and ns * ne * rows * dim * 2 <= 8 << 20 and own * ff_bytes(expert_gate) <= 12 << 20
    mixer_out, tokens = mixer_call(
        ns, ne, dense, lo, lift, maps, writes, result_valve_maps, norm_gain[None, :], output_weight, residual,
        post_gain[None, :], route_experts, route_weights, lanes,
    )
    if not dense:
        return mixer_out, routed(tokens, route_experts, route_weights, expert_gate, expert_up, expert_down)
    return mixer_out, expert_call(ns, ne, tokens, expert_gate, expert_up, expert_down)


def ff_bytes(weight):
    return 3 * weight.shape[1] * weight.shape[2] * 2


def solution(mesh):
    in_specs = (
        P("seq", "exp"),
        P("seq", "exp"),
        P("seq", "exp"),
        P("seq", "exp"),
        P("seq", "exp"),
        P("seq", "exp"),
        P("exp"),
        P(None, "exp"),
        P(None, "exp"),
        P(None, "exp"),
        P(),
        P("exp", None),
        P(("seq", "exp"), None),
        P(),
        P(("seq", "exp"), None),
        P(("seq", "exp"), None),
        P(("seq", "exp"), None, None),
        P(("seq", "exp"), None, None),
        P(("seq", "exp"), None, None),
    )
    out_specs = (P(("seq", "exp"), None), P(("seq", "exp"), None))
    return jax.shard_map(body, mesh=mesh, in_specs=in_specs, out_specs=out_specs, check_vma=False)
```
